32 devices in a mesh: tm: 4 (over y, x), stn: 8 (over z, core).
Axes of the slice: x: 2, y: 2, z: 4, core: 2. Of those that a mesh axis runs over, the one named last changes fastest.
Arguments:
- voltages: bfloat16 [256, 262144], P('stn', 'tm'), may hold values from -6 to 6
- gains: float32 [2, 256, 256], P(None, 'stn'), may hold values from -4 to 4
Outputs:
- visibility: float32 [256, 2, 256, 256], P(('tm', 'stn'))
The draws below stay inside these ranges and needn't reach their ends.
All inputs are finite; a program needn't handle non-finite values.
Results may differ from the reference program's by a relative error of at most 0.0038.
Values may be sent and summed in bfloat16 or wider, within the bound.
A program may use at most 128 MiB of HBM per device.

```python
import jax
import jax.numpy as jnp
from jax import lax

CHANNELS = 4096
BAND = 256
BAND_LOW = 1024
TAPS = 8
INPUTS = 256
FRAMES = 32
SAMPLES = 262144


def block_levels(key, dims, shards, least, top_value):
    def one(dim, parts):
        heights = jax.random.uniform(jax.random.fold_in(jax.random.fold_in(key, 6), dim), (parts,), jnp.float32, least / len(shards), top_value / len(shards))
        return jnp.repeat(jnp.exp(heights), dims[dim] // parts).reshape((-1,) + (1,) * (len(dims) - dim - 1))

    level = one(*shards[0])
    for cut in shards[1:]:
        level = level * one(*cut)
    return level


def normal_values(rng, dims, deviation, reach, pieces=(), held_as=jnp.bfloat16):
    level = block_levels(rng, dims, pieces, -0.22, 0.18) if pieces else 1.0
    entries = jax.random.normal(rng, dims, jnp.float32) * deviation * level
    return jnp.minimum(jnp.maximum(entries, -reach), reach).astype(held_as)


def setup_inputs(seed: int = 0) -> dict:
    seeds = jax.random.split(jax.random.key(seed), 3)
    voltages = normal_values(seeds[0], (INPUTS, SAMPLES), 1.0, 6.0, ((0, 8), (1, 4)))
    gains = normal_values(seeds[1], (2, INPUTS, BAND), 0.7, 4.0, ((1, 8),), jnp.float32)
    return dict(voltages=voltages, gains=gains)


def window_table(chans):
    frame_len = 2 * chans
    total_len = TAPS * frame_len
    positions = jnp.arange(total_len, dtype=jnp.float32)
    centred = (positions - (total_len - 1) / 2.0) / frame_len
    taper = jnp.sin(jnp.pi * (positions + 0.5) / total_len)
    shaped = jnp.sinc(centred) * taper * taper
    shaped = shaped / jnp.sqrt(jnp.sum(shaped * shaped))
    return shaped.reshape(TAPS, frame_len)

def reference(voltages, gains):
    frame_len = 2 * CHANNELS
    window = window_table(CHANNELS)

    def one_input(operands):
        row_data, gain_rows = operands
        padded = jnp.concatenate([jnp.zeros(((TAPS - 1) * frame_len,), row_data.dtype), row_data])
        framed = padded.reshape(FRAMES + TAPS - 1, frame_len).astype(jnp.float32)
        windowed = jnp.zeros((FRAMES, frame_len), jnp.float32)
        for tap_index in range(TAPS):
            windowed = windowed + window[tap_index] * framed[tap_index:tap_index + FRAMES]
        spectrum = jnp.fft.rfft(windowed, axis=1)[:, BAND_LOW:BAND_LOW + BAND]
        real_part = jnp.real(spectrum).astype(jnp.float32)
        imag_part = jnp.imag(spectrum).astype(jnp.float32)
        gain_real = gain_rows[0][None, :]
        gain_imag = gain_rows[1][None, :]
        scaled_real = gain_real * real_part - gain_imag * imag_part
        scaled_imag = gain_real * imag_part + gain_imag * real_part
        return jnp.stack([scaled_real, scaled_imag]).astype(jnp.bfloat16)
    spectra = lax.map(one_input, (voltages, jnp.transpose(gains, (1, 0, 2))))
    block = min(16, BAND)
    starts = (jnp.arange(BAND // block) * block).astype(jnp.int32)

    def one_block(start):
        piece = lax.dynamic_slice_in_dim(spectra, start, block, 3).astype(jnp.float32)
        real_part = piece[:, 0]
        imag_part = piece[:, 1]
        vis_real = jnp.einsum('ifc,jfc->cij', real_part, real_part) + jnp.einsum('ifc,jfc->cij', imag_part, imag_part)
        vis_imag = jnp.einsum('ifc,jfc->cij', imag_part, real_part) - jnp.einsum('ifc,jfc->cij', real_part, imag_part)
        return jnp.stack([vis_real, vis_imag], axis=1) / FRAMES
    blocks_out = lax.map(one_block, starts)
    return blocks_out.reshape(BAND, 2, INPUTS, INPUTS)
```

```python
import functools

import jax
import jax.numpy as jnp
import numpy as np
from jax import lax
from jax.experimental import pallas as pl
from jax.experimental.pallas import tpu as pltpu
from jax.sharding import PartitionSpec as P

CHANNELS = 4096
BAND_LOW = 1024
TAPS = 8


def passed_along(x, axis, by):
    devices = lax.axis_size(axis)
    pairs = [(i, i + by) for i in range(devices) if 0 <= i + by < devices]
    return lax.ppermute(x, axis, pairs)


def window_table(chans):
    frame_len = 2 * chans
    total_len = TAPS * frame_len
    positions = jnp.arange(total_len, dtype=jnp.float32)
    centred = (positions - (total_len - 1) / 2.0) / frame_len
    taper = jnp.sin(jnp.pi * (positions + 0.5) / total_len)
    shaped = jnp.sinc(centred) * taper * taper
    shaped = shaped / jnp.sqrt(jnp.sum(shaped * shaped))
    return shaped.reshape(TAPS, frame_len)


def band_tables(frame_len, band):
    sample_index = jnp.arange(frame_len, dtype=jnp.int32)[:, None]
    channel_index = (BAND_LOW + jnp.arange(band, dtype=jnp.int32))[None, :]
    phase = (sample_index * channel_index % frame_len).astype(jnp.float32)
    angles = 2.0 * jnp.pi * phase / frame_len
    return (jnp.cos(angles), jnp.sin(angles))


def band_spectra(windowed, cos_table, sin_table):
    highest = lax.Precision.HIGHEST
    real_part = jnp.einsum("ifm,mk->kif", windowed, cos_table, precision=highest)
    imag_part = -jnp.einsum("ifm,mk->kif", windowed, sin_table, precision=highest)
    return (real_part, imag_part)


def apply_taps(window, extended, frames):
    windowed = jnp.zeros((extended.shape[0], frames, extended.shape[2]), jnp.float32)
    for tap_index in range(TAPS):
        windowed = windowed + window[tap_index] * extended[
            :, tap_index : tap_index + frames, :
        ].astype(jnp.float32)
    return windowed


def operands(turned):
    stacked = jnp.concatenate([turned[0], turned[1]], axis=-1)
    flipped = jnp.concatenate([turned[1], -turned[0]], axis=-1)
    return (stacked, flipped)


def cross_power(stacked, flipped, total_frames):
    vis_real = jnp.einsum("cif,cjf->cij", stacked, stacked, preferred_element_type=jnp.float32)
    vis_imag = jnp.einsum("cif,cjf->cij", flipped, stacked, preferred_element_type=jnp.float32)
    return jnp.stack([vis_real, vis_imag], axis=1) / total_frames


def on_device(voltages, gains):
    in_dev, length = voltages.shape
    band = gains.shape[2]
    frame_len = 2 * CHANNELS
    frames = length // frame_len
    n_time = lax.axis_size("tm")
    n_station = lax.axis_size("stn")
    per_device = band // (n_time * n_station)
    all_inputs = in_dev * n_station
    history = TAPS - 1
    window = window_table(CHANNELS)
    cos_table, sin_table = band_tables(frame_len, band)
    framed = voltages.reshape(in_dev, frames, frame_len)
    before = passed_along(framed[:, frames - history :, :], "tm", 1)
    extended = jnp.concatenate([before, framed], axis=1)
    windowed = apply_taps(window, extended, frames)
    raw_real, raw_imag = band_spectra(windowed, cos_table, sin_table)
    gain_real = jnp.transpose(gains[0])[:, :, None]
    gain_imag = jnp.transpose(gains[1])[:, :, None]
    spec_real = gain_real * raw_real - gain_imag * raw_imag
    spec_imag = gain_real * raw_imag + gain_imag * raw_real
    spectra = jnp.stack([spec_real, spec_imag]).astype(jnp.bfloat16)
    blocks = spectra.reshape(2, n_time, n_station, per_device, in_dev, frames)
    turned = lax.all_to_all(
        lax.all_to_all(blocks, "tm", split_axis=1, concat_axis=5, tiled=True),
        "stn",
        split_axis=2,
        concat_axis=4,
        tiled=True,
    )
    turned = turned.reshape(2, per_device, all_inputs, n_time * frames)
    stacked, flipped = operands(turned)
    return cross_power(stacked, flipped, float(n_time * frames))


HALO = jnp.float32
CHUNK = 512
LANES = 128


def host_window(chans):
    frame_len = 2 * chans
    total = TAPS * frame_len
    n = np.arange(total, dtype=np.float64)
    raw = np.sinc((n - (total - 1) / 2) / frame_len)
    raw = raw * np.sin(np.pi * (n + 0.5) / total) ** 2
    return (raw / np.sqrt(np.sum(raw * raw))).reshape(TAPS, frame_len).astype(np.float32)


def host_tables(chans, band, owners):
    frame_len = 2 * chans
    m = np.arange(chans, dtype=np.int64)[:, None]
    parts = []
    for parity in range(2):
        c = BAND_LOW + np.arange(parity, band, 2, dtype=np.int64)[None, :]
        angle = 2.0 * np.pi * ((m * c) % frame_len) / frame_len
        parts.append(np.concatenate([np.cos(angle), -np.sin(angle)], axis=1))
    full = np.stack(parts)
    high = full.astype(np.float32).astype(jnp.bfloat16)
    low = (full - high.astype(np.float64)).astype(np.float32).astype(jnp.bfloat16)
    return np.stack([high, low])


def taps_into(v_ref, w_ref, x_ref, base, in_dev, frames, halo):
    rows = in_dev * (frames - 1 if halo else frames)
    for tile in range(CHUNK // LANES):
        at = pl.multiple_of(base + tile * LANES, LANES)
        here = slice(tile * LANES, (tile + 1) * LANES)
        for part in range(in_dev // 16):
            who = slice(part * 16, part * 16 + 16)
            halves = []
            for half in range(2):
                v = [
                    v_ref[2 * f + half, who, pl.ds(at, LANES)].astype(jnp.float32)
                    for f in range(frames)
                ]
                w = [w_ref[half, pl.ds(p, 1), pl.ds(at, LANES)] for p in range(TAPS)]
                sums = []
                if halo:
                    for j in range(frames - 1):
                        sums.append(sum(w[p] * v[j + 1 + p] for p in range(TAPS - 1 - j)))
                else:
                    for f in range(frames):
                        sums.append(sum(w[TAPS - 1 - q] * v[f - q] for q in range(f + 1)))
                halves.append(sums)
            for f in range(len(halves[0])):
                for parity in range(2):
                    a, b = halves[0][f], halves[1][f]
                    x = a - b if parity else a + b
                    high = x.astype(jnp.bfloat16)
                    low = (x - high.astype(jnp.float32)).astype(jnp.bfloat16)
                    r = f * in_dev + part * 16
                    x_ref[parity, r : r + 16, here] = high
                    x_ref[parity, rows + r : rows + r + 16, here] = low


def transform(x_ref, t_ref, acc_ref, base, rows):
    at = pl.multiple_of(base, CHUNK)
    for parity in range(2):
        x = x_ref[parity, 0 : 2 * rows, :]
        th = t_ref[0, parity, pl.ds(at, CHUNK), :]
        tl = t_ref[1, parity, pl.ds(at, CHUNK), :]
        both = jnp.dot(x, th, preferred_element_type=jnp.float32)
        extra = jnp.dot(x[:rows], tl, preferred_element_type=jnp.float32)
        acc_ref[parity, 0:rows, :] += both[:rows] + both[rows:] + extra


def swap_blocks(arrays, block):
    lane = lax.broadcasted_iota(jnp.int32, arrays[0].shape, 1)
    step = 1
    while step < len(arrays):
        low = (lane // (block * step)) % 2 == 0
        shift = block * step
        out = list(arrays)
        for q in range(len(arrays)):
            if q & step == 0:
                a, b = arrays[q], arrays[q | step]
                out[q] = jnp.where(low, a, pltpu.roll(b, shift, 1))
                out[q | step] = jnp.where(low, pltpu.roll(a, LANES - shift, 1), b)
        arrays = out
        step *= 2
    return arrays


def spectra_kernel(
    n_time, n_station, frames,
    v_hbm, w_hbm, t_hbm, g_ref, got_ref,
    v_ref, w_ref, t_ref, x0, x1, acc, hsend, hrecv, send, gain,
    v_sem, w_sem, t_sem, h_sem, send_sem, recv_sem,
):
    me_t, me_s = lax.axis_index("tm"), lax.axis_index("stn")
    n_dev = n_time * n_station
    me = me_t * n_station + me_s
    in_dev, half_len = v_ref.shape[1], v_ref.shape[2]
    chunks = half_len // CHUNK
    barrier = pltpu.get_barrier_semaphore()

    def greet(o, carry):
        to = lax.rem(me + o, n_dev)
        pl.semaphore_signal(
            barrier, inc=1, device_id=(to // n_station, lax.rem(to, n_station)),
            device_id_type=pl.DeviceIdType.MESH,
        )
        return carry

    lax.fori_loop(1, n_dev, greet, 0)

    def v_copy(c, i):
        at = pl.multiple_of(c * CHUNK, CHUNK)
        src = pl.multiple_of(i * half_len + c * CHUNK, CHUNK)
        return pltpu.make_async_copy(
            v_hbm.at[:, pl.ds(src, CHUNK)], v_ref.at[i, :, pl.ds(at, CHUNK)], v_sem.at[c, i]
        )

    def t_copy(c):
        at = pl.multiple_of(c * CHUNK, CHUNK)
        return pltpu.make_async_copy(
            t_hbm.at[:, :, pl.ds(at, CHUNK), :], t_ref.at[:, :, pl.ds(at, CHUNK), :], t_sem.at[c]
        )

    w_copy = pltpu.make_async_copy(w_hbm, w_ref, w_sem)
    w_copy.start()

    def begin(c, carry):
        lax.fori_loop(0, 2 * frames, lambda i, k: (v_copy(c, i).start(), k)[1], 0)
        t_copy(c).start()
        return carry

    lax.fori_loop(0, chunks, begin, 0)
    acc[...] = jnp.zeros_like(acc)

    def arrived(c):
        lax.fori_loop(0, 2 * frames, lambda i, k: (v_copy(c, i).wait(), k)[1], 0)
        t_copy(c).wait()

    def sweep(halo):
        rows = in_dev * (frames - 1 if halo else frames)

        def taps(c, x):
            taps_into(v_ref, w_ref, x, c * CHUNK, in_dev, frames, halo)

        if halo:
            arrived(0)
        taps(0, x0)

        def pair(k, carry):
            c = 2 * k
            if halo:
                arrived(c + 1)

                @pl.when(c + 2 < chunks)
                def _():
                    arrived(c + 2)

            taps(c + 1, x1)
            transform(x0, t_ref, acc, c * CHUNK, rows)
            taps(jnp.minimum(c + 2, chunks - 1), x0)
            transform(x1, t_ref, acc, (c + 1) * CHUNK, rows)
            return carry

        lax.fori_loop(0, chunks // 2, pair, 0)

    w_copy.wait()
    sweep(True)
    hrows = in_dev * (frames - 1)
    for parity in range(2):
        hsend[parity] = acc[parity, 0:hrows, :].astype(hsend.dtype)
    pl.semaphore_wait(barrier, n_dev - 1)
    onward = pltpu.make_async_remote_copy(
        src_ref=hsend, dst_ref=hrecv, send_sem=h_sem.at[0], recv_sem=h_sem.at[1],
        device_id=(lax.rem(me_t + 1, n_time), me_s), device_id_type=pl.DeviceIdType.MESH,
    )

    @pl.when(me_t < n_time - 1)
    def _():
        onward.start()

    acc[...] = jnp.zeros_like(acc)
    band = g_ref.shape[2]
    row = lax.broadcasted_iota(jnp.int32, (band, band), 0)
    col = lax.broadcasted_iota(jnp.int32, (band, band), 1)
    pick = (row == 2 * lax.rem(col, band // 2) + col // (band // 2)).astype(jnp.float32)
    for reim in range(2):
        gain[reim] = jnp.dot(
            g_ref[reim], pick, precision=lax.Precision.HIGHEST, preferred_element_type=jnp.float32
        )
    sweep(False)

    @pl.when(me_t > 0)
    def _():
        onward.wait_recv()
        for parity in range(2):
            acc[parity, 0:hrows, :] += hrecv[parity].astype(jnp.float32)

    half = band // 2
    for part in range(in_dev // 16):
        who = slice(part * 16, part * 16 + 16)
        arrays = []
        for parity in range(2):
            gr = gain[0, who, parity * half : (parity + 1) * half]
            gi = gain[1, who, parity * half : (parity + 1) * half]
            res, ims = [], []
            for f in range(frames):
                r = f * in_dev + part * 16
                re = acc[parity, r : r + 16, 0:half]
                im = acc[parity, r : r + 16, half:band]
                res.append(gr * re - gi * im)
                ims.append(gr * im + gi * re)
            arrays += res + ims
        arrays = swap_blocks(arrays, LANES // len(arrays))
        for d in range(n_dev):
            send[d, who, :] = arrays[d].astype(jnp.bfloat16)
    got_ref[me] = send[me]

    def outgoing(o):
        to = lax.rem(me + o, n_dev)
        return pltpu.make_async_remote_copy(
            src_ref=send.at[to], dst_ref=got_ref.at[me],
            send_sem=send_sem.at[o], recv_sem=recv_sem.at[me],
            device_id=(to // n_station, lax.rem(to, n_station)),
            device_id_type=pl.DeviceIdType.MESH,
        )

    def incoming(o):
        src = lax.rem(me + o, n_dev)
        return pltpu.make_async_remote_copy(
            src_ref=send.at[src], dst_ref=got_ref.at[src],
            send_sem=send_sem.at[o], recv_sem=recv_sem.at[src],
            device_id=(src // n_station, lax.rem(src, n_station)),
            device_id_type=pl.DeviceIdType.MESH,
        )

    lax.fori_loop(1, n_dev, lambda o, k: (outgoing(o).start(), k)[1], 0)
    lax.fori_loop(1, n_dev, lambda o, k: (incoming(o).wait_recv(), k)[1], 0)
    lax.fori_loop(1, n_dev, lambda o, k: (outgoing(o).wait_send(), k)[1], 0)

    @pl.when(me_t < n_time - 1)
    def _():
        onward.wait_send()


def correlate_kernel(n_time, got_ref, out_ref, a_ref, b_ref):
    c = pl.program_id(0)
    inputs = out_ref.shape[2]
    reach = LANES // 4

    @pl.when(c == 0)
    def _():
        for t in range(n_time):
            here = slice(t * LANES, (t + 1) * LANES)
            a = got_ref[t * inputs : (t + 1) * inputs, :]
            wide = a.astype(jnp.float32)
            lane = lax.broadcasted_iota(jnp.int32, wide.shape, 1)
            real = (lane // reach) % 2 == 0
            turned = jnp.where(
                real, pltpu.roll(wide, LANES - reach, 1), -pltpu.roll(wide, reach, 1)
            )
            a_ref[0:inputs, here] = a
            a_ref[inputs : 2 * inputs, here] = turned.astype(jnp.bfloat16)

    lane = lax.rem(lax.broadcasted_iota(jnp.int32, (1, n_time * LANES), 1), LANES)
    mine = (lane // (LANES // 2) == lax.rem(c, 2)) & (lax.rem(lane, 4) == c // 2)
    mask = jnp.where(mine, 1.0, 0.0).astype(jnp.bfloat16)
    b_ref[...] = a_ref[0:inputs, :] * mask
    power = lax.dot_general(
        a_ref[...], b_ref[...], (((1,), (1,)), ((), ())), preferred_element_type=jnp.float32
    )
    power = power * (1.0 / (8 * n_time))
    out_ref[0, 0] = power[:inputs]
    out_ref[0, 1] = power[inputs:]


def on_device_fast(voltages, gains):
    in_dev, length = voltages.shape
    band = gains.shape[2]
    frame_len = 2 * CHANNELS
    frames = length // frame_len
    n_time = lax.axis_size("tm")
    n_station = lax.axis_size("stn")
    n_dev = n_time * n_station
    inputs = in_dev * n_station
    hrows = in_dev * (frames - 1)
    rows = in_dev * frames
    window = host_window(CHANNELS).reshape(TAPS, 2, CHANNELS).transpose(1, 0, 2)
    tables = host_tables(CHANNELS, band, n_dev)
    chunks = CHANNELS // CHUNK
    any_space = pl.BlockSpec(memory_space=pl.ANY)
    vmem = pl.BlockSpec(memory_space=pltpu.VMEM)
    got = pl.pallas_call(
        functools.partial(spectra_kernel, n_time, n_station, frames),
        out_shape=jax.ShapeDtypeStruct((n_dev, in_dev, LANES), jnp.bfloat16),
        in_specs=[any_space, any_space, any_space, vmem],
        out_specs=vmem,
        scratch_shapes=[
            pltpu.VMEM((2 * frames, in_dev, CHANNELS), jnp.bfloat16),
            pltpu.VMEM((2, TAPS, CHANNELS), jnp.float32),
            pltpu.VMEM((2, 2, CHANNELS, band), jnp.bfloat16),
            pltpu.VMEM((2, 2 * rows, CHUNK), jnp.bfloat16),
            pltpu.VMEM((2, 2 * rows, CHUNK), jnp.bfloat16),
            pltpu.VMEM((2, rows, band), jnp.float32),
            pltpu.VMEM((2, hrows, band), HALO),
            pltpu.VMEM((2, hrows, band), HALO),
            pltpu.VMEM((n_dev, in_dev, LANES), jnp.bfloat16),
            pltpu.VMEM((2, in_dev, band), jnp.float32),
            pltpu.SemaphoreType.DMA((chunks, 2 * frames)),
            pltpu.SemaphoreType.DMA,
            pltpu.SemaphoreType.DMA((chunks,)),
            pltpu.SemaphoreType.DMA((2,)),
            pltpu.SemaphoreType.DMA((n_dev,)),
            pltpu.SemaphoreType.DMA((n_dev,)),
        ],
        compiler_params=pltpu.CompilerParams(
            collective_id=0, has_side_effects=True, vmem_limit_bytes=48 * 2**20
        ),
        name="spectra",
    )(voltages, window, tables, gains)
    per_device = band // n_dev
    return pl.pallas_call(
        functools.partial(correlate_kernel, n_time),
        grid=(per_device,),
        out_shape=jax.ShapeDtypeStruct((per_device, 2, inputs, inputs), jnp.float32),
        in_specs=[pl.BlockSpec((n_time * inputs, LANES), lambda c: (0, 0))],
        out_specs=pl.BlockSpec((1, 2, inputs, inputs), lambda c: (c, 0, 0, 0)),
        scratch_shapes=[
            pltpu.VMEM((2 * inputs, n_time * LANES), jnp.bfloat16),
            pltpu.VMEM((inputs, n_time * LANES), jnp.bfloat16),
        ],
        compiler_params=pltpu.CompilerParams(vmem_limit_bytes=32 * 2**20),
        name="correlate",
    )(got.reshape(n_time * inputs, LANES))


def solution(mesh):
    in_specs = (P("stn", "tm"), P(None, "stn", None))
    out_specs = P(("tm", "stn"), None, None, None)

    def body(voltages, gains):
        n_dev = mesh.shape["tm"] * mesh.shape["stn"]
        frames = voltages.shape[1] // (2 * CHANNELS)
        if 2 * frames * (gains.shape[2] // n_dev) == LANES and frames == TAPS:
            return on_device_fast(voltages, gains)
        return on_device(voltages, gains)

    return jax.shard_map(
        body, mesh=mesh, in_specs=in_specs, out_specs=out_specs, check_vma=False
    )
```

```python
import functools

import jax
import jax.numpy as jnp
import numpy as np
from jax import lax
from jax.experimental import pallas as pl
from jax.experimental.pallas import tpu as pltpu
from jax.sharding import PartitionSpec as P

CHANNELS = 4096
BAND_LOW = 1024
TAPS = 8


def passed_along(x, axis, by):
    devices = lax.axis_size(axis)
    pairs = [(i, i + by) for i in range(devices) if 0 <= i + by < devices]
    return lax.ppermute(x, axis, pairs)


def window_table(chans):
    frame_len = 2 * chans
    total_len = TAPS * frame_len
    positions = jnp.arange(total_len, dtype=jnp.float32)
    centred = (positions - (total_len - 1) / 2.0) / frame_len
    taper = jnp.sin(jnp.pi * (positions + 0.5) / total_len)
    shaped = jnp.sinc(centred) * taper * taper
    shaped = shaped / jnp.sqrt(jnp.sum(shaped * shaped))
    return shaped.reshape(TAPS, frame_len)


def band_tables(frame_len, band):
    sample_index = jnp.arange(frame_len, dtype=jnp.int32)[:, None]
    channel_index = (BAND_LOW + jnp.arange(band, dtype=jnp.int32))[None, :]
    phase = (sample_index * channel_index % frame_len).astype(jnp.float32)
    angles = 2.0 * jnp.pi * phase / frame_len
    return (jnp.cos(angles), jnp.sin(angles))


def band_spectra(windowed, cos_table, sin_table):
    highest = lax.Precision.HIGHEST
    real_part = jnp.einsum("ifm,mk->kif", windowed, cos_table, precision=highest)
    imag_part = -jnp.einsum("ifm,mk->kif", windowed, sin_table, precision=highest)
    return (real_part, imag_part)


def apply_taps(window, extended, frames):
    windowed = jnp.zeros((extended.shape[0], frames, extended.shape[2]), jnp.float32)
    for tap_index in range(TAPS):
        windowed = windowed + window[tap_index] * extended[
            :, tap_index : tap_index + frames, :
        ].astype(jnp.float32)
    return windowed


def operands(turned):
    stacked = jnp.concatenate([turned[0], turned[1]], axis=-1)
    flipped = jnp.concatenate([turned[1], -turned[0]], axis=-1)
    return (stacked, flipped)


def cross_power(stacked, flipped, total_frames):
    vis_real = jnp.einsum("cif,cjf->cij", stacked, stacked, preferred_element_type=jnp.float32)
    vis_imag = jnp.einsum("cif,cjf->cij", flipped, stacked, preferred_element_type=jnp.float32)
    return jnp.stack([vis_real, vis_imag], axis=1) / total_frames


def on_device(voltages, gains):
    in_dev, length = voltages.shape
    band = gains.shape[2]
    frame_len = 2 * CHANNELS
    frames = length // frame_len
    n_time = lax.axis_size("tm")
    n_station = lax.axis_size("stn")
    per_device = band // (n_time * n_station)
    all_inputs = in_dev * n_station
    history = TAPS - 1
    window = window_table(CHANNELS)
    cos_table, sin_table = band_tables(frame_len, band)
    framed = voltages.reshape(in_dev, frames, frame_len)
    before = passed_along(framed[:, frames - history :, :], "tm", 1)
    extended = jnp.concatenate([before, framed], axis=1)
    windowed = apply_taps(window, extended, frames)
    raw_real, raw_imag = band_spectra(windowed, cos_table, sin_table)
    gain_real = jnp.transpose(gains[0])[:, :, None]
    gain_imag = jnp.transpose(gains[1])[:, :, None]
    spec_real = gain_real * raw_real - gain_imag * raw_imag
    spec_imag = gain_real * raw_imag + gain_imag * raw_real
    spectra = jnp.stack([spec_real, spec_imag]).astype(jnp.bfloat16)
    blocks = spectra.reshape(2, n_time, n_station, per_device, in_dev, frames)
    turned = lax.all_to_all(
        lax.all_to_all(blocks, "tm", split_axis=1, concat_axis=5, tiled=True),
        "stn",
        split_axis=2,
        concat_axis=4,
        tiled=True,
    )
    turned = turned.reshape(2, per_device, all_inputs, n_time * frames)
    stacked, flipped = operands(turned)
    return cross_power(stacked, flipped, float(n_time * frames))


CHUNK = 512
LANES = 128


def host_window(chans):
    frame_len = 2 * chans
    total = TAPS * frame_len
    n = np.arange(total, dtype=np.float64)
    raw = np.sinc((n - (total - 1) / 2) / frame_len)
    raw = raw * np.sin(np.pi * (n + 0.5) / total) ** 2
    return (raw / np.sqrt(np.sum(raw * raw))).reshape(TAPS, frame_len).astype(np.float32)


def host_tables(chans, band, owners):
    frame_len = 2 * chans
    m = np.arange(chans, dtype=np.int64)[:, None]
    parts = []
    for parity in range(2):
        c = BAND_LOW + np.arange(parity, band, 2, dtype=np.int64)[None, :]
        angle = 2.0 * np.pi * ((m * c) % frame_len) / frame_len
        parts.append(np.concatenate([np.cos(angle), -np.sin(angle)], axis=1))
    full = np.stack(parts)
    high = full.astype(np.float32).astype(jnp.bfloat16)
    low = (full - high.astype(np.float64)).astype(np.float32).astype(jnp.bfloat16)
    return np.stack([high, low])


def taps_into(v_ref, w_ref, x_ref, base, in_dev, frames, halo):
    rows = in_dev * (frames - 1 if halo else frames)
    for tile in range(CHUNK // LANES):
        at = pl.multiple_of(base + tile * LANES, LANES)
        for part in range(in_dev // 16):
            who = slice(part * 16, part * 16 + 16)
            halves = []
            for half in range(2):
                v = [
                    v_ref[2 * f + half, who, pl.ds(at, LANES)].astype(jnp.float32)
                    for f in range(frames)
                ]
                w = [w_ref[half, pl.ds(p, 1), pl.ds(at, LANES)] for p in range(TAPS)]
                sums = []
                if halo:
                    for j in range(frames - 1):
                        sums.append(sum(w[p] * v[j + 1 + p] for p in range(TAPS - 1 - j)))
                else:
                    for f in range(frames):
                        sums.append(sum(w[TAPS - 1 - q] * v[f - q] for q in range(f + 1)))
                halves.append(sums)
            for f in range(len(halves[0])):
                for parity in range(2):
                    a, b = halves[0][f], halves[1][f]
                    x = a - b if parity else a + b
                    high = x.astype(jnp.bfloat16)
                    low = (x - high.astype(jnp.float32)).astype(jnp.bfloat16)
                    r = f * in_dev + part * 16
                    x_ref[parity, r : r + 16, pl.ds(at, LANES)] = high
                    x_ref[parity, rows + r : rows + r + 16, pl.ds(at, LANES)] = low


def transform(x_ref, t_ref, acc_ref, parity, base, depth, rows):
    at = pl.ds(pl.multiple_of(base, depth), depth)
    x = x_ref[parity, 0 : 2 * rows, at]
    both = jnp.dot(x, t_ref[0, parity, at, :], preferred_element_type=jnp.float32)
    extra = jnp.dot(x[:rows], t_ref[1, parity, at, :], preferred_element_type=jnp.float32)
    acc_ref[parity] += both[:rows] + both[rows:] + extra


def swap_blocks(arrays, block):
    lane = lax.broadcasted_iota(jnp.int32, arrays[0].shape, 1)
    step = 1
    while step < len(arrays):
        low = (lane // (block * step)) % 2 == 0
        shift = block * step
        out = list(arrays)
        for q in range(len(arrays)):
            if q & step == 0:
                a, b = arrays[q], arrays[q | step]
                out[q] = jnp.where(low, a, pltpu.roll(b, shift, 1))
                out[q | step] = jnp.where(low, pltpu.roll(a, LANES - shift, 1), b)
        arrays = out
        step *= 2
    return arrays


def spectra_kernel(
    n_time, n_station, frames,
    v_hbm, w_hbm, t_hbm, g_ref, got_ref,
    v_ref, w_ref, t_ref, hx, x, hacc, acc, hrecv, send, gain,
    v_sem, w_sem, t_sem, hs_sem, hr_sem, send_sem, recv_sem,
):
    me_t, me_s = lax.axis_index("tm"), lax.axis_index("stn")
    n_dev = n_time * n_station
    me = me_t * n_station + me_s
    in_dev, half_len = v_ref.shape[1], v_ref.shape[2]
    chunks = half_len // CHUNK
    rows, hrows = in_dev * frames, in_dev * (frames - 1)
    first = 2 * CHUNK
    spans = (slice(0, first), slice(first, half_len))

    def v_copy(g, i):
        return pltpu.make_async_copy(
            v_hbm.at[:, i * half_len + spans[g].start : i * half_len + spans[g].stop],
            v_ref.at[i, :, spans[g]],
            v_sem.at[g, i],
        )

    def t_copy(g, parity):
        return pltpu.make_async_copy(
            t_hbm.at[:, parity, spans[g], :], t_ref.at[:, parity, spans[g], :], t_sem.at[g, parity]
        )

    w_copy = pltpu.make_async_copy(w_hbm, w_ref, w_sem)
    w_copy.start()
    for g in range(2):
        for i in range(2 * frames):
            v_copy(g, i).start()
        t_copy(g, 0).start()
    for g in range(2):
        t_copy(g, 1).start()

    barrier = pltpu.get_barrier_semaphore()

    def greet(o, carry):
        to = lax.rem(me + o, n_dev)
        pl.semaphore_signal(
            barrier, inc=1, device_id=(to // n_station, lax.rem(to, n_station)),
            device_id_type=pl.DeviceIdType.MESH,
        )
        return carry

    lax.fori_loop(1, n_dev, greet, 0)
    hacc[...] = jnp.zeros_like(hacc)
    acc[...] = jnp.zeros_like(acc)

    band = g_ref.shape[2]
    half = band // 2
    row = lax.broadcasted_iota(jnp.int32, (band, band), 0)
    col = lax.broadcasted_iota(jnp.int32, (band, band), 1)
    pick = (row == 2 * lax.rem(col, half) + col // half).astype(jnp.float32)
    for reim in range(2):
        gain[reim] = jnp.dot(
            g_ref[reim], pick, precision=lax.Precision.HIGHEST, preferred_element_type=jnp.float32
        )

    def arrived(g):
        for i in range(2 * frames):
            v_copy(g, i).wait()
        t_copy(g, 0).wait()

    def taps(c, halo):
        taps_into(v_ref, w_ref, hx if halo else x, c * CHUNK, in_dev, frames, halo)

    def onward(parity):
        return pltpu.make_async_remote_copy(
            src_ref=hacc.at[parity], dst_ref=hrecv.at[parity],
            send_sem=hs_sem.at[parity], recv_sem=hr_sem.at[parity],
            device_id=(lax.rem(me_t + 1, n_time), me_s), device_id_type=pl.DeviceIdType.MESH,
        )

    def pass_on(parity):
        @pl.when(me_t < n_time - 1)
        def _():
            onward(parity).start()

    def outgoing(parity, o):
        to = lax.rem(me + o, n_dev)
        return pltpu.make_async_remote_copy(
            src_ref=send.at[parity, to], dst_ref=got_ref.at[parity, me],
            send_sem=send_sem.at[parity, o], recv_sem=recv_sem.at[parity, me],
            device_id=(to // n_station, lax.rem(to, n_station)),
            device_id_type=pl.DeviceIdType.MESH,
        )

    def incoming(parity, o):
        src = lax.rem(me + o, n_dev)
        return pltpu.make_async_remote_copy(
            src_ref=send.at[parity, src], dst_ref=got_ref.at[parity, src],
            send_sem=send_sem.at[parity, o], recv_sem=recv_sem.at[parity, src],
            device_id=(src // n_station, lax.rem(src, n_station)),
            device_id_type=pl.DeviceIdType.MESH,
        )

    def hand_out(parity):
        @pl.when(me_t > 0)
        def _():
            onward(parity).wait_recv()
            acc[parity, 0:hrows, :] += hrecv[parity]

        arrays = []
        for part in range(in_dev // 16):
            who = slice(part * 16, part * 16 + 16)
            gr = gain[0, who, parity * half : (parity + 1) * half]
            gi = gain[1, who, parity * half : (parity + 1) * half]
            res, ims = [], []
            for f in range(frames):
                r = f * in_dev + part * 16
                re = acc[parity, r : r + 16, 0:half]
                im = acc[parity, r : r + 16, half:band]
                res.append(gr * re - gi * im)
                ims.append(gr * im + gi * re)
            arrays += res + ims
        arrays = swap_blocks(arrays, LANES // len(arrays))
        for d in range(n_dev):
            send[parity, d] = arrays[d].astype(jnp.bfloat16)
        lax.fori_loop(1, n_dev, lambda o, k: (outgoing(parity, o).start(), k)[1], 0)
        got_ref[parity, me] = send[parity, me]

    w_copy.wait()
    arrived(0)
    taps(0, True)
    taps(1, True)
    transform(hx, t_ref, hacc, 0, 0, CHUNK, hrows)
    arrived(1)

    def stage(c, carry):
        taps(c + 1, True)
        transform(hx, t_ref, hacc, 0, c * CHUNK, CHUNK, hrows)
        return carry

    lax.fori_loop(1, chunks - 1, stage, 0)
    transform(hx, t_ref, hacc, 0, (chunks - 1) * CHUNK, CHUNK, hrows)
    pl.semaphore_wait(barrier, n_dev - 1)
    pass_on(0)
    for g in range(2):
        t_copy(g, 1).wait()

    def stage_odd(c, carry):
        taps(c, False)
        transform(hx, t_ref, hacc, 1, c * CHUNK, CHUNK, hrows)
        return carry

    lax.fori_loop(0, chunks, stage_odd, 0)
    pass_on(1)
    for parity in range(2):

        def own(c, carry):
            transform(x, t_ref, acc, parity, c * 2 * CHUNK, 2 * CHUNK, rows)
            return carry

        lax.fori_loop(0, chunks // 2, own, 0)
        hand_out(parity)

    for parity in range(2):
        lax.fori_loop(1, n_dev, lambda o, k: (incoming(parity, o).wait_recv(), k)[1], 0)
        lax.fori_loop(1, n_dev, lambda o, k: (outgoing(parity, o).wait_send(), k)[1], 0)

        @pl.when(me_t < n_time - 1)
        def _():
            onward(parity).wait_send()


def correlate_kernel(n_time, n_station, got_ref, out_hbm, a_ref, out_ref, out_sem):
    inputs = out_ref.shape[2]
    group = 16
    side, reach = LANES // 2, LANES // 4
    wide_shape = (n_station * group, LANES)
    lane = lax.broadcasted_iota(jnp.int32, wide_shape, 1)
    is_low, is_real = lane < side, (lane // reach) % 2 == 0
    scale = 1.0 / (TAPS * n_time)
    copies = []
    for parity in range(2):
        for two in range(n_time // 2):
            g0, g1 = [
                got_ref[parity, t * n_station : (t + 1) * n_station]
                .astype(jnp.float32)
                .reshape(wide_shape)
                for t in (2 * two, 2 * two + 1)
            ]
            here = slice(two * LANES, (two + 1) * LANES)
            for part in range(2):
                if part == 0:
                    a = jnp.where(is_low, g0, pltpu.roll(g1, side, 1))
                else:
                    a = jnp.where(is_low, pltpu.roll(g0, side, 1), g1)
                turned = jnp.where(
                    is_real, pltpu.roll(a, LANES - reach, 1), -pltpu.roll(a, reach, 1)
                )
                for i, rows in ((0, a), (inputs, turned)):
                    rows = rows.astype(jnp.bfloat16)
                    for s in range(n_station):
                        to = i + (2 * s + part) * group
                        a_ref[parity, to : to + group, here] = rows[s * group : (s + 1) * group]
        width = n_time * side
        pair = lax.rem(lax.broadcasted_iota(jnp.int32, (1, width), 1), 4)
        for u in range(out_ref.shape[0] // 2):
            mask = jnp.where(pair == u, scale, 0.0).astype(jnp.bfloat16)
            power = lax.dot_general(
                a_ref[parity], a_ref[parity, 0:inputs, :] * mask, (((1,), (1,)), ((), ())),
                preferred_element_type=jnp.float32,
            )
            c = 2 * u + parity
            out_ref[c, 0] = power[:inputs]
            out_ref[c, 1] = power[inputs:]
            copy = pltpu.make_async_copy(out_ref.at[c], out_hbm.at[c], out_sem.at[c])
            copy.start()
            copies.append(copy)
    for copy in copies:
        copy.wait()


def on_device_fast(voltages, gains):
    in_dev, length = voltages.shape
    band = gains.shape[2]
    frame_len = 2 * CHANNELS
    frames = length // frame_len
    n_time = lax.axis_size("tm")
    n_station = lax.axis_size("stn")
    n_dev = n_time * n_station
    inputs = in_dev * n_station
    hrows = in_dev * (frames - 1)
    rows = in_dev * frames
    window = host_window(CHANNELS).reshape(TAPS, 2, CHANNELS).transpose(1, 0, 2)
    tables = host_tables(CHANNELS, band, n_dev)
    any_space = pl.BlockSpec(memory_space=pl.ANY)
    vmem = pl.BlockSpec(memory_space=pltpu.VMEM)
    got = pl.pallas_call(
        functools.partial(spectra_kernel, n_time, n_station, frames),
        out_shape=jax.ShapeDtypeStruct((2, n_dev, in_dev // 2, LANES), jnp.bfloat16),
        in_specs=[any_space, any_space, any_space, vmem],
        out_specs=vmem,
        scratch_shapes=[
            pltpu.VMEM((2 * frames, in_dev, CHANNELS), jnp.bfloat16),
            pltpu.VMEM((2, TAPS, CHANNELS), jnp.float32),
            pltpu.VMEM((2, 2, CHANNELS, band), jnp.bfloat16),
            pltpu.VMEM((2, 2 * hrows, CHANNELS), jnp.bfloat16),
            pltpu.VMEM((2, 2 * rows, CHANNELS), jnp.bfloat16),
            pltpu.VMEM((2, hrows, band), jnp.float32),
            pltpu.VMEM((2, rows, band), jnp.float32),
            pltpu.VMEM((2, hrows, band), jnp.float32),
            pltpu.VMEM((2, n_dev, in_dev // 2, LANES), jnp.bfloat16),
            pltpu.VMEM((2, in_dev, band), jnp.float32),
            pltpu.SemaphoreType.DMA((2, 2 * frames)),
            pltpu.SemaphoreType.DMA,
            pltpu.SemaphoreType.DMA((2, 2)),
            pltpu.SemaphoreType.DMA((2,)),
            pltpu.SemaphoreType.DMA((2,)),
            pltpu.SemaphoreType.DMA((2, n_dev)),
            pltpu.SemaphoreType.DMA((2, n_dev)),
        ],
        compiler_params=pltpu.CompilerParams(
            collective_id=0, has_side_effects=True, vmem_limit_bytes=61 * 2**20
        ),
        name="spectra",
    )(voltages, window, tables, gains)
    per_device = band // n_dev
    return pl.pallas_call(
        functools.partial(correlate_kernel, n_time, n_station),
        out_shape=jax.ShapeDtypeStruct((per_device, 2, inputs, inputs), jnp.float32),
        in_specs=[vmem],
        out_specs=any_space,
        scratch_shapes=[
            pltpu.VMEM((2, 2 * inputs, n_time * LANES // 2), jnp.bfloat16),
            pltpu.VMEM((per_device, 2, inputs, inputs), jnp.float32),
            pltpu.SemaphoreType.DMA((per_device,)),
        ],
        compiler_params=pltpu.CompilerParams(vmem_limit_bytes=48 * 2**20),
        name="correlate",
    )(got)


def solution(mesh):
    in_specs = (P("stn", "tm"), P(None, "stn", None))
    out_specs = P(("tm", "stn"), None, None, None)

    def body(voltages, gains):
        n_dev = mesh.shape["tm"] * mesh.shape["stn"]
        frames = voltages.shape[1] // (2 * CHANNELS)
        if 2 * frames * (gains.shape[2] // n_dev) == LANES and frames == TAPS and voltages.shape[0] == 32:
            return on_device_fast(voltages, gains)
        return on_device(voltages, gains)

    return jax.shard_map(
        body, mesh=mesh, in_specs=in_specs, out_specs=out_specs, check_vma=False
    )
```

```python
import functools

import jax
import jax.numpy as jnp
import numpy as np
from jax import lax
from jax.experimental import pallas as pl
from jax.experimental.pallas import tpu as pltpu
from jax.sharding import PartitionSpec as P

CHANNELS = 4096
BAND_LOW = 1024
TAPS = 8


def passed_along(x, axis, by):
    devices = lax.axis_size(axis)
    pairs = [(i, i + by) for i in range(devices) if 0 <= i + by < devices]
    return lax.ppermute(x, axis, pairs)


def window_table(chans):
    frame_len = 2 * chans
    total_len = TAPS * frame_len
    positions = jnp.arange(total_len, dtype=jnp.float32)
    centred = (positions - (total_len - 1) / 2.0) / frame_len
    taper = jnp.sin(jnp.pi * (positions + 0.5) / total_len)
    shaped = jnp.sinc(centred) * taper * taper
    shaped = shaped / jnp.sqrt(jnp.sum(shaped * shaped))
    return shaped.reshape(TAPS, frame_len)


def band_tables(frame_len, band):
    sample_index = jnp.arange(frame_len, dtype=jnp.int32)[:, None]
    channel_index = (BAND_LOW + jnp.arange(band, dtype=jnp.int32))[None, :]
    phase = (sample_index * channel_index % frame_len).astype(jnp.float32)
    angles = 2.0 * jnp.pi * phase / frame_len
    return (jnp.cos(angles), jnp.sin(angles))


def band_spectra(windowed, cos_table, sin_table):
    highest = lax.Precision.HIGHEST
    real_part = jnp.einsum("ifm,mk->kif", windowed, cos_table, precision=highest)
    imag_part = -jnp.einsum("ifm,mk->kif", windowed, sin_table, precision=highest)
    return (real_part, imag_part)


def apply_taps(window, extended, frames):
    windowed = jnp.zeros((extended.shape[0], frames, extended.shape[2]), jnp.float32)
    for tap_index in range(TAPS):
        windowed = windowed + window[tap_index] * extended[
            :, tap_index : tap_index + frames, :
        ].astype(jnp.float32)
    return windowed


def operands(turned):
    stacked = jnp.concatenate([turned[0], turned[1]], axis=-1)
    flipped = jnp.concatenate([turned[1], -turned[0]], axis=-1)
    return (stacked, flipped)


def cross_power(stacked, flipped, total_frames):
    vis_real = jnp.einsum("cif,cjf->cij", stacked, stacked, preferred_element_type=jnp.float32)
    vis_imag = jnp.einsum("cif,cjf->cij", flipped, stacked, preferred_element_type=jnp.float32)
    return jnp.stack([vis_real, vis_imag], axis=1) / total_frames


def on_device(voltages, gains):
    in_dev, length = voltages.shape
    band = gains.shape[2]
    frame_len = 2 * CHANNELS
    frames = length // frame_len
    n_time = lax.axis_size("tm")
    n_station = lax.axis_size("stn")
    per_device = band // (n_time * n_station)
    all_inputs = in_dev * n_station
    history = TAPS - 1
    window = window_table(CHANNELS)
    cos_table, sin_table = band_tables(frame_len, band)
    framed = voltages.reshape(in_dev, frames, frame_len)
    before = passed_along(framed[:, frames - history :, :], "tm", 1)
    extended = jnp.concatenate([before, framed], axis=1)
    windowed = apply_taps(window, extended, frames)
    raw_real, raw_imag = band_spectra(windowed, cos_table, sin_table)
    gain_real = jnp.transpose(gains[0])[:, :, None]
    gain_imag = jnp.transpose(gains[1])[:, :, None]
    spec_real = gain_real * raw_real - gain_imag * raw_imag
    spec_imag = gain_real * raw_imag + gain_imag * raw_real
    spectra = jnp.stack([spec_real, spec_imag]).astype(jnp.bfloat16)
    blocks = spectra.reshape(2, n_time, n_station, per_device, in_dev, frames)
    turned = lax.all_to_all(
        lax.all_to_all(blocks, "tm", split_axis=1, concat_axis=5, tiled=True),
        "stn",
        split_axis=2,
        concat_axis=4,
        tiled=True,
    )
    turned = turned.reshape(2, per_device, all_inputs, n_time * frames)
    stacked, flipped = operands(turned)
    return cross_power(stacked, flipped, float(n_time * frames))


CHUNK = 512
LANES = 128


def host_window(chans):
    frame_len = 2 * chans
    total = TAPS * frame_len
    n = np.arange(total, dtype=np.float64)
    raw = np.sinc((n - (total - 1) / 2) / frame_len)
    raw = raw * np.sin(np.pi * (n + 0.5) / total) ** 2
    return (raw / np.sqrt(np.sum(raw * raw))).reshape(TAPS, frame_len).astype(np.float32)


def host_tables(chans, band, owners):
    frame_len = 2 * chans
    m = np.arange(chans, dtype=np.int64)[:, None]
    parts = []
    for parity in range(2):
        c = BAND_LOW + np.arange(parity, band, 2, dtype=np.int64)[None, :]
        angle = 2.0 * np.pi * ((m * c) % frame_len) / frame_len
        parts.append(np.concatenate([np.cos(angle), -np.sin(angle)], axis=1))
    full = np.stack(parts)
    high = full.astype(np.float32).astype(jnp.bfloat16)
    low = (full - high.astype(np.float64)).astype(np.float32).astype(jnp.bfloat16)
    return np.stack([high, low])


def taps_into(v_ref, w_ref, x_ref, base, in_dev, frames, halo):
    rows = in_dev * (frames - 1 if halo else frames)
    for tile in range(CHUNK // LANES):
        at = pl.multiple_of(base + tile * LANES, LANES)
        into = slice(tile * LANES, (tile + 1) * LANES)
        for part in range(in_dev // 16):
            who = slice(part * 16, part * 16 + 16)
            halves = []
            for half in range(2):
                v = [
                    v_ref[2 * f + half, who, pl.ds(at, LANES)].astype(jnp.float32)
                    for f in range(frames)
                ]
                w = [w_ref[half, pl.ds(p, 1), pl.ds(at, LANES)] for p in range(TAPS)]
                sums = []
                if halo:
                    for j in range(frames - 1):
                        sums.append(sum(w[p] * v[j + 1 + p] for p in range(TAPS - 1 - j)))
                else:
                    for f in range(frames):
                        sums.append(sum(w[TAPS - 1 - q] * v[f - q] for q in range(f + 1)))
                halves.append(sums)
            for f in range(len(halves[0])):
                for parity in range(2):
                    a, b = halves[0][f], halves[1][f]
                    x = a - b if parity else a + b
                    high = x.astype(jnp.bfloat16)
                    low = (x - high.astype(jnp.float32)).astype(jnp.bfloat16)
                    r = f * in_dev + part * 16
                    x_ref[parity, r : r + 16, into] = high
                    x_ref[parity, rows + r : rows + r + 16, into] = low


def transform(x_ref, t_ref, acc_ref, parity, base, depth, rows):
    at = pl.ds(pl.multiple_of(base, depth), depth)
    x = x_ref[parity]
    both = jnp.dot(x, t_ref[0, parity, at, :], preferred_element_type=jnp.float32)
    extra = jnp.dot(x[:rows], t_ref[1, parity, at, :], preferred_element_type=jnp.float32)
    acc_ref[parity] += both[:rows] + both[rows:] + extra


def swap_blocks(arrays, block):
    lane = lax.broadcasted_iota(jnp.int32, arrays[0].shape, 1)
    step = 1
    while step < len(arrays):
        low = (lane // (block * step)) % 2 == 0
        shift = block * step
        out = list(arrays)
        for q in range(len(arrays)):
            if q & step == 0:
                a, b = arrays[q], arrays[q | step]
                out[q] = jnp.where(low, a, pltpu.roll(b, shift, 1))
                out[q | step] = jnp.where(low, pltpu.roll(a, LANES - shift, 1), b)
        arrays = out
        step *= 2
    return arrays


def spectra_kernel(
    n_time, n_station, frames,
    v_hbm, w_hbm, t_hbm, g_ref, got_ref,
    v_ref, w_ref, t_ref, hx0, hx1, x, hacc, acc, hrecv, send, gain,
    v_sem, w_sem, t_sem, hs_sem, hr_sem, send_sem, recv_sem,
):
    me_t, me_s = lax.axis_index("tm"), lax.axis_index("stn")
    n_dev = n_time * n_station
    me = me_t * n_station + me_s
    in_dev, half_len = v_ref.shape[1], v_ref.shape[2]
    chunks = half_len // CHUNK
    rows, hrows = in_dev * frames, in_dev * (frames - 1)
    first = 2 * CHUNK
    spans = (slice(0, first), slice(first, half_len))

    def v_copy(g, i):
        return pltpu.make_async_copy(
            v_hbm.at[:, i * half_len + spans[g].start : i * half_len + spans[g].stop],
            v_ref.at[i, :, spans[g]],
            v_sem.at[g, i],
        )

    def t_copy(g, parity):
        return pltpu.make_async_copy(
            t_hbm.at[:, parity, spans[g], :], t_ref.at[:, parity, spans[g], :], t_sem.at[g, parity]
        )

    w_copy = pltpu.make_async_copy(w_hbm, w_ref, w_sem)
    w_copy.start()
    for g in range(2):
        for i in range(2 * frames):
            v_copy(g, i).start()
        t_copy(g, 0).start()
    for g in range(2):
        t_copy(g, 1).start()

    barrier = pltpu.get_barrier_semaphore()

    def greet(o, carry):
        to = lax.rem(me + o, n_dev)
        pl.semaphore_signal(
            barrier, inc=1, device_id=(to // n_station, lax.rem(to, n_station)),
            device_id_type=pl.DeviceIdType.MESH,
        )
        return carry

    lax.fori_loop(1, n_dev, greet, 0)
    hacc[...] = jnp.zeros_like(hacc)
    acc[...] = jnp.zeros_like(acc)

    band = g_ref.shape[2]
    half = band // 2
    row = lax.broadcasted_iota(jnp.int32, (band, band), 0)
    col = lax.broadcasted_iota(jnp.int32, (band, band), 1)
    pick = (row == 2 * lax.rem(col, half) + col // half).astype(jnp.float32)
    for reim in range(2):
        gain[reim] = jnp.dot(
            g_ref[reim], pick, precision=lax.Precision.HIGHEST, preferred_element_type=jnp.float32
        )

    def arrived(g):
        for i in range(2 * frames):
            v_copy(g, i).wait()
        t_copy(g, 0).wait()

    def taps(c):
        taps_into(v_ref, w_ref, x.at[c], c * CHUNK, in_dev, frames, False)

    def halo_taps(k, odd):
        taps_into(
            v_ref, w_ref, (hx0, hx1)[odd].at[k], (2 * k + odd) * CHUNK, in_dev, frames, True
        )

    def halo_dots(parity, k, odd):
        c = (2 * k + odd) * CHUNK
        transform((hx0, hx1)[odd].at[k], t_ref, hacc, parity, c, CHUNK, hrows)

    def onward(parity):
        return pltpu.make_async_remote_copy(
            src_ref=hacc.at[parity], dst_ref=hrecv.at[parity],
            send_sem=hs_sem.at[parity], recv_sem=hr_sem.at[parity],
            device_id=(lax.rem(me_t + 1, n_time), me_s), device_id_type=pl.DeviceIdType.MESH,
        )

    def pass_on(parity):
        @pl.when(me_t < n_time - 1)
        def _():
            onward(parity).start()

    def outgoing(parity, o):
        to = lax.rem(me + o, n_dev)
        return pltpu.make_async_remote_copy(
            src_ref=send.at[parity, to], dst_ref=got_ref.at[parity, me],
            send_sem=send_sem.at[parity, o], recv_sem=recv_sem.at[parity, me],
            device_id=(to // n_station, lax.rem(to, n_station)),
            device_id_type=pl.DeviceIdType.MESH,
        )

    def incoming(parity, o):
        src = lax.rem(me + o, n_dev)
        return pltpu.make_async_remote_copy(
            src_ref=send.at[parity, src], dst_ref=got_ref.at[parity, src],
            send_sem=send_sem.at[parity, o], recv_sem=recv_sem.at[parity, src],
            device_id=(src // n_station, lax.rem(src, n_station)),
            device_id_type=pl.DeviceIdType.MESH,
        )

    def hand_out(parity):
        @pl.when(me_t > 0)
        def _():
            onward(parity).wait_recv()
            acc[parity, 0:hrows, :] += hrecv[parity]

        arrays = []
        for part in range(in_dev // 16):
            who = slice(part * 16, part * 16 + 16)
            gr = gain[0, who, parity * half : (parity + 1) * half]
            gi = gain[1, who, parity * half : (parity + 1) * half]
            res, ims = [], []
            for f in range(frames):
                r = f * in_dev + part * 16
                re = acc[parity, r : r + 16, 0:half]
                im = acc[parity, r : r + 16, half:band]
                res.append(gr * re - gi * im)
                ims.append(gr * im + gi * re)
            arrays += res + ims
        arrays = swap_blocks(arrays, LANES // len(arrays))
        for d in range(n_dev):
            send[parity, d] = arrays[d].astype(jnp.bfloat16)
        lax.fori_loop(1, n_dev, lambda o, k: (outgoing(parity, o).start(), k)[1], 0)
        got_ref[parity, me] = send[parity, me]

    w_copy.wait()
    arrived(0)
    halo_taps(0, 0)
    halo_taps(0, 1)
    halo_dots(0, 0, 0)
    arrived(1)

    def stage(k, carry):
        halo_taps(k, 0)
        halo_dots(0, k - 1, 1)
        halo_taps(k, 1)
        halo_dots(0, k, 0)
        return carry

    lax.fori_loop(1, chunks // 2, stage, 0)
    halo_dots(0, chunks // 2 - 1, 1)
    pl.semaphore_wait(barrier, n_dev - 1)
    pass_on(0)
    for g in range(2):
        t_copy(g, 1).wait()

    def stage_odd(k, carry):
        for odd in range(2):
            taps(2 * k + odd)
            halo_dots(1, k, odd)
        return carry

    lax.fori_loop(0, chunks // 2, stage_odd, 0)
    pass_on(1)
    for parity in range(2):

        def own(c, carry):
            transform(x.at[c], t_ref, acc, parity, c * CHUNK, CHUNK, rows)
            return carry

        lax.fori_loop(0, chunks, own, 0)
        hand_out(parity)

    for parity in range(2):
        lax.fori_loop(1, n_dev, lambda o, k: (incoming(parity, o).wait_recv(), k)[1], 0)
        lax.fori_loop(1, n_dev, lambda o, k: (outgoing(parity, o).wait_send(), k)[1], 0)

        @pl.when(me_t < n_time - 1)
        def _():
            onward(parity).wait_send()


def correlate_kernel(n_time, n_station, got_ref, out_hbm, a_ref, out_ref, out_sem):
    inputs = out_ref.shape[2]
    group = 16
    side, reach = LANES // 2, LANES // 4
    wide_shape = (n_station * group, LANES)
    lane = lax.broadcasted_iota(jnp.int32, wide_shape, 1)
    is_low, is_real = lane < side, (lane // reach) % 2 == 0
    scale = 1.0 / (TAPS * n_time)
    copies = []
    for parity in range(2):
        for two in range(n_time // 2):
            g0, g1 = [
                got_ref[parity, t * n_station : (t + 1) * n_station]
                .astype(jnp.float32)
                .reshape(wide_shape)
                for t in (2 * two, 2 * two + 1)
            ]
            here = slice(two * LANES, (two + 1) * LANES)
            for part in range(2):
                if part == 0:
                    a = jnp.where(is_low, g0, pltpu.roll(g1, side, 1))
                else:
                    a = jnp.where(is_low, pltpu.roll(g0, side, 1), g1)
                turned = jnp.where(
                    is_real, pltpu.roll(a, LANES - reach, 1), -pltpu.roll(a, reach, 1)
                )
                for i, rows in ((0, a), (inputs, turned)):
                    rows = rows.astype(jnp.bfloat16)
                    for s in range(n_station):
                        to = i + (2 * s + part) * group
                        a_ref[parity, to : to + group, here] = rows[s * group : (s + 1) * group]
        width = n_time * side
        pair = lax.rem(lax.broadcasted_iota(jnp.int32, (1, width), 1), 4)
        for u in range(out_ref.shape[0] // 2):
            mask = jnp.where(pair == u, scale, 0.0).astype(jnp.bfloat16)
            power = lax.dot_general(
                a_ref[parity], a_ref[parity, 0:inputs, :] * mask, (((1,), (1,)), ((), ())),
                preferred_element_type=jnp.float32,
            )
            c = 2 * u + parity
            out_ref[c, 0] = power[:inputs]
            out_ref[c, 1] = power[inputs:]
            copy = pltpu.make_async_copy(out_ref.at[c], out_hbm.at[c], out_sem.at[c])
            copy.start()
            copies.append(copy)
    for copy in copies:
        copy.wait()


def on_device_fast(voltages, gains):
    in_dev, length = voltages.shape
    band = gains.shape[2]
    frame_len = 2 * CHANNELS
    frames = length // frame_len
    n_time = lax.axis_size("tm")
    n_station = lax.axis_size("stn")
    n_dev = n_time * n_station
    inputs = in_dev * n_station
    hrows = in_dev * (frames - 1)
    rows = in_dev * frames
    window = host_window(CHANNELS).reshape(TAPS, 2, CHANNELS).transpose(1, 0, 2)
    tables = host_tables(CHANNELS, band, n_dev)
    any_space = pl.BlockSpec(memory_space=pl.ANY)
    vmem = pl.BlockSpec(memory_space=pltpu.VMEM)
    got = pl.pallas_call(
        functools.partial(spectra_kernel, n_time, n_station, frames),
        out_shape=jax.ShapeDtypeStruct((2, n_dev, in_dev // 2, LANES), jnp.bfloat16),
        in_specs=[any_space, any_space, any_space, vmem],
        out_specs=vmem,
        scratch_shapes=[
            pltpu.VMEM((2 * frames, in_dev, CHANNELS), jnp.bfloat16),
            pltpu.VMEM((2, TAPS, CHANNELS), jnp.float32),
            pltpu.VMEM((2, 2, CHANNELS, band), jnp.bfloat16),
            pltpu.VMEM((CHANNELS // CHUNK // 2, 2, 2 * hrows, CHUNK), jnp.bfloat16),
            pltpu.VMEM((CHANNELS // CHUNK // 2, 2, 2 * hrows, CHUNK), jnp.bfloat16),
            pltpu.VMEM((CHANNELS // CHUNK, 2, 2 * rows, CHUNK), jnp.bfloat16),
            pltpu.VMEM((2, hrows, band), jnp.float32),
            pltpu.VMEM((2, rows, band), jnp.float32),
            pltpu.VMEM((2, hrows, band), jnp.float32),
            pltpu.VMEM((2, n_dev, in_dev // 2, LANES), jnp.bfloat16),
            pltpu.VMEM((2, in_dev, band), jnp.float32),
            pltpu.SemaphoreType.DMA((2, 2 * frames)),
            pltpu.SemaphoreType.DMA,
            pltpu.SemaphoreType.DMA((2, 2)),
            pltpu.SemaphoreType.DMA((2,)),
            pltpu.SemaphoreType.DMA((2,)),
            pltpu.SemaphoreType.DMA((2, n_dev)),
            pltpu.SemaphoreType.DMA((2, n_dev)),
        ],
        compiler_params=pltpu.CompilerParams(
            collective_id=0, has_side_effects=True, vmem_limit_bytes=61 * 2**20
        ),
        name="spectra",
    )(voltages, window, tables, gains)
    per_device = band // n_dev
    return pl.pallas_call(
        functools.partial(correlate_kernel, n_time, n_station),
        out_shape=jax.ShapeDtypeStruct((per_device, 2, inputs, inputs), jnp.float32),
        in_specs=[vmem],
        out_specs=any_space,
        scratch_shapes=[
            pltpu.VMEM((2, 2 * inputs, n_time * LANES // 2), jnp.bfloat16),
            pltpu.VMEM((per_device, 2, inputs, inputs), jnp.float32),
            pltpu.SemaphoreType.DMA((per_device,)),
        ],
        compiler_params=pltpu.CompilerParams(vmem_limit_bytes=48 * 2**20),
        name="correlate",
    )(got)


def solution(mesh):
    in_specs = (P("stn", "tm"), P(None, "stn", None))
    out_specs = P(("tm", "stn"), None, None, None)

    def body(voltages, gains):
        n_dev = mesh.shape["tm"] * mesh.shape["stn"]
        frames = voltages.shape[1] // (2 * CHANNELS)
        if 2 * frames * (gains.shape[2] // n_dev) == LANES and frames == TAPS and voltages.shape[0] == 32:
            return on_device_fast(voltages, gains)
        return on_device(voltages, gains)

    return jax.shard_map(
        body, mesh=mesh, in_specs=in_specs, out_specs=out_specs, check_vma=False
    )
```
